32 devices in a mesh: ctx: 8 (over z, x), tp: 4 (over y, core).
Axes of the slice: x: 2, y: 2, z: 4, core: 2. Of those that a mesh axis runs over, the one named last changes fastest.
Arguments:
- projected: bfloat16 [3, 4096, 8192], P(None, 'ctx', 'tp'), may hold values from -6 to 6
- short_filter: float32 [3, 3, 8192], P(None, None, 'tp'), may hold values from -3.5 to 3.5
- long_filter: bfloat16 [128, 8192], P(None, 'tp'), may hold values from -0.5 to 0.5
- skip_gain: float32 [8192], P('tp'), may hold values from -3 to 3
- out_weight: bfloat16 [8192, 8192], P('tp', 'ctx'), may hold values from -0.0625 to 0.0625
- out_grad: bfloat16 [4096, 8192], P('ctx'), may hold values from -6 to 6
- left_source: int32 [8], replicated, may hold values from -1 to 7, as said below
Outputs:
- mixed: bfloat16 [4096, 8192], P(('ctx', 'tp'))
- grad_projected: bfloat16 [3, 4096, 8192], P(None, 'ctx', 'tp')
- grad_long: float32 [128, 8192], P(None, 'tp')
- grad_short: float32 [3, 3, 8192], P(None, None, 'tp')
The draws below stay inside these ranges and needn't reach their ends.
Inputs may be any that keep to these rules, and one draw needn't show every extreme that they name: left_source[b] is -1 where block b begins a contig, else another block; no block is named by two blocks, and following left_source from any block ends at -1 without repeating a block.
All inputs are finite; a program needn't handle non-finite values.
Results may differ from the reference program's by a relative error of at most 0.015.
Values may be sent and summed in bfloat16 or wider, within the bound.
A program may use at most 192 MiB of HBM per device.

```python
import math
import jax
import jax.numpy as jnp
from jax import lax

D = 8192
FILT = 128
SHORT = 3
TOK_DEV = 512
TOKENS = 4096
N_CTX = 8
N_TP = 4


def draw_left_source(key, part):
    perm_key, link_key = jax.random.split(jax.random.fold_in(key, 7))
    positions = jnp.arange(N_CTX, dtype=jnp.int32)
    placed = jax.random.permutation(perm_key, N_CTX).astype(jnp.int32)
    logical = jnp.zeros((N_CTX,), jnp.int32).at[placed].set(positions)
    last_place = logical[N_CTX - 1]
    swapped = placed.at[N_CTX - 1].set(placed[N_CTX - 2]).at[N_CTX - 2].set(placed[N_CTX - 1])
    placed = jnp.where(last_place == N_CTX - 1, swapped, placed)
    logical = jnp.zeros((N_CTX,), jnp.int32).at[placed].set(positions)
    forced = logical[N_CTX - 1] + 1
    linked = (jax.random.randint(link_key, (N_CTX,), 0, 3) > 0) | (positions == forced)
    linked = linked & (positions > 0)
    previous = jnp.roll(placed, 1)
    values = jnp.where(linked, previous, -1).astype(jnp.int32)
    return jnp.zeros((N_CTX,), jnp.int32).at[placed].set(values)


def steps_of(stream_key, extent, cuts, least, top_value):
    gain, own = 1.0, jax.random.fold_in(stream_key, 6)
    for dim, shards_of in cuts:
        heights = jnp.exp(jax.random.uniform(jax.random.fold_in(own, dim), (shards_of,), jnp.float32, least / len(cuts), top_value / len(cuts)))
        gain = gain * jnp.repeat(heights, extent[dim] // shards_of).reshape([-1 if axis == dim else 1 for axis in range(len(extent))])
    return gain


def normal_values(key, shape, deviation, reach, cuts=(), kind=jnp.bfloat16):
    entries = jax.random.normal(key, shape, jnp.float32) * deviation
    if len(cuts) > 0:
        entries = steps_of(key, shape, cuts, -0.22, 0.18) * entries
    return jnp.clip(entries, min=-reach, max=reach).astype(kind)


def setup_inputs(seed: int = 0) -> dict:
    streams_of = jax.random.split(jax.random.key(seed), 8)
    return {
        "projected": normal_values(streams_of[0], (3, TOKENS, D), 1.0, 6.0, ((1, 8), (2, 4))),
        "short_filter": normal_values(streams_of[1], (3, SHORT, D), SHORT ** -0.5, 3.5, ((2, 4),), jnp.float32),
        "long_filter": normal_values(streams_of[2], (FILT, D), FILT ** -0.5, 0.5, ((1, 4),)),
        "skip_gain": normal_values(streams_of[3], (D,), 0.5, 3.0, ((0, 4),), jnp.float32),
        "out_weight": normal_values(streams_of[4], (D, D), D ** -0.5, 0.0625, ((0, 4), (1, 8))),
        "out_grad": normal_values(streams_of[5], (TOKENS, D), 1.0, 6.0, ((0, 8),)),
        "left_source": draw_left_source(jax.random.fold_in(streams_of[7], 71), 0),
    }


def extend_left(values, edge_rows, source, has_left):
    tail = jnp.take(values[..., values.shape[-2] - edge_rows:, :], source, axis=-3)
    tail = jnp.where(has_left[:, None, None], tail, jnp.zeros_like(tail))
    return jnp.concatenate([tail, values], axis=-2)

def extend_right(values, edge_rows, reader, has_right):
    head = jnp.take(values[..., :edge_rows, :], reader, axis=-3)
    head = jnp.where(has_right[:, None, None], head, jnp.zeros_like(head))
    return jnp.concatenate([values, head], axis=-2)

def toeplitz_ref(filt_taps, block_rows):
    lag_index = jnp.arange(block_rows)[:, None] + FILT - jnp.arange(block_rows + FILT)[None, :]
    inside = (lag_index >= 0) & (lag_index < FILT)
    picked = jnp.take(filt_taps, jnp.clip(lag_index, 0, FILT - 1), axis=0)
    return jnp.where(inside[:, :, None], picked, jnp.zeros_like(picked))

def windows_ref(extended, block_rows):
    shape = extended.shape
    block_count = (shape[1] - FILT) // block_rows
    blocks = extended.reshape(shape[0], shape[1] // block_rows, block_rows, shape[2])
    pieces = [blocks[:, offset:offset + block_count] for offset in range(FILT // block_rows + 1)]
    return jnp.concatenate(pieces, axis=2)

def causal_ref(extended, filt_taps):
    block_rows = FILT // 2
    toeplitz = toeplitz_ref(filt_taps, block_rows)
    windows = windows_ref(extended, block_rows)
    result = jnp.einsum('ijc,brjc->bric', toeplitz, windows, precision=lax.Precision.HIGHEST)
    return result.reshape(extended.shape[0], -1, extended.shape[2])

def lag_ref(grad_conv, extended):
    block_rows = FILT // 2
    windows = windows_ref(extended, block_rows)
    shape = grad_conv.shape
    blocks = grad_conv.reshape(shape[0], shape[1] // block_rows, block_rows, shape[2])
    product = jnp.einsum('bric,brjc->ijc', blocks, windows, precision=lax.Precision.HIGHEST)
    lag_index = jnp.arange(block_rows)[:, None] + FILT - jnp.arange(FILT)[None, :]
    picked = product[jnp.arange(block_rows)[:, None], lag_index]
    return lax.optimization_barrier(jnp.sum(picked, axis=0))

def reference(projected, short_filter, long_filter, skip_gain, out_weight, out_grad, left_source):
    block_total = left_source.shape[0]
    positions = jnp.arange(block_total, dtype=jnp.int32)
    has_left = left_source >= 0
    source = jnp.maximum(left_source, 0).astype(jnp.int32)
    is_reader = left_source[None, :] == positions[:, None]
    has_right = jnp.any(is_reader, axis=1)
    reader = lax.optimization_barrier(jnp.sum(jnp.where(is_reader, positions[None, :], 0), axis=1)).astype(jnp.int32)
    channels = D // N_TP
    edge_rows = SHORT - 1
    grad_scale = 1.0 / math.sqrt(TOKENS)

    def one_group(out_accum, group_index):
        first_chan = group_index * channels
        streams = lax.dynamic_slice_in_dim(projected, first_chan, channels, 2)
        streams = streams.reshape(3, block_total, TOK_DEV, channels).astype(jnp.float32)
        tap_weights = lax.dynamic_slice_in_dim(short_filter, first_chan, channels, 2)
        filt_taps = lax.dynamic_slice_in_dim(long_filter, first_chan, channels, 1).astype(jnp.float32)
        skip_row = lax.dynamic_slice_in_dim(skip_gain, first_chan, channels, 0)
        weight_rows = lax.dynamic_slice_in_dim(out_weight, first_chan, channels, 0)
        streams_ext = extend_left(streams, edge_rows, source, has_left)
        act = jnp.zeros((3, block_total, TOK_DEV, channels), jnp.float32)
        for shift in range(SHORT):
            act = act + tap_weights[:, shift][:, None, None, :] * streams_ext[:, :, edge_rows - shift:edge_rows - shift + TOK_DEV]
        mixin = (act[1] * act[2]).astype(jnp.bfloat16)
        mixin_wide = mixin.astype(jnp.float32)
        mixin_ext = extend_left(mixin_wide, FILT, source, has_left)
        conv = causal_ref(mixin_ext, filt_taps) + skip_row * mixin_wide
        gated = (act[0] * conv).astype(jnp.bfloat16)
        partial_out = jnp.dot(gated.reshape(TOKENS, channels), weight_rows, preferred_element_type=jnp.float32)
        out_accum = out_accum + partial_out
        back_grad = jnp.dot(out_grad, weight_rows.T, preferred_element_type=jnp.float32)
        back_grad = back_grad.reshape(block_total, TOK_DEV, channels)
        grad_conv = (back_grad * act[0]).astype(jnp.bfloat16)
        grad_gate = back_grad * conv
        grad_wide = grad_conv.astype(jnp.float32)
        grad_ext = extend_right(grad_wide, FILT, reader, has_right)
        grad_mixin = jnp.flip(causal_ref(jnp.flip(grad_ext, 1), filt_taps), 1) + skip_row * grad_wide
        grad_act = jnp.stack([grad_gate, grad_mixin * act[2], grad_mixin * act[1]])
        grad_act_ext = extend_right(grad_act, edge_rows, reader, has_right)
        grad_streams = jnp.zeros((3, block_total, TOK_DEV, channels), jnp.float32)
        for shift in range(SHORT):
            grad_streams = grad_streams + tap_weights[:, shift][:, None, None, :] * grad_act_ext[:, :, shift:shift + TOK_DEV]
        short_terms = jnp.stack([lax.optimization_barrier(jnp.sum(grad_act * streams_ext[:, :, edge_rows - shift:edge_rows - shift + TOK_DEV], axis=(1, 2))) for shift in range(SHORT)], axis=1)
        long_terms = lag_ref(grad_wide, mixin_ext)
        grad_streams = grad_streams.reshape(3, TOKENS, channels).astype(jnp.bfloat16)
        return (out_accum, (grad_streams, long_terms * grad_scale, short_terms * grad_scale))
    out_accum, outputs = lax.scan(one_group, jnp.zeros((TOKENS, D), jnp.float32), jnp.arange(N_TP, dtype=jnp.int32))
    grad_streams, long_terms, short_terms = outputs
    grad_projected = jnp.transpose(grad_streams, (1, 2, 0, 3)).reshape(3, TOKENS, D)
    grad_long = jnp.transpose(long_terms, (1, 0, 2)).reshape(FILT, D)
    grad_short = jnp.transpose(short_terms, (1, 2, 0, 3)).reshape(3, SHORT, D)
    return (out_accum.astype(jnp.bfloat16), grad_projected, grad_long, grad_short)
```

```python
import math

import jax
import jax.numpy as jnp
from jax import lax
from jax.sharding import PartitionSpec as P

edge_depth = 8
chunk_count = 4
head_pad = 16


def short_forward(extended, tap_weights, out_rows):
    summed = jnp.zeros((extended.shape[0], out_rows, extended.shape[2]), jnp.float32)
    for shift in range(tap_weights.shape[1]):
        piece = extended[:, edge_depth - shift : edge_depth - shift + out_rows].astype(jnp.float32)
        summed = summed + tap_weights[:, shift][:, None, :] * piece
    return summed


def depthwise(signal, kernel):
    channels = signal.shape[1]
    result = lax.conv_general_dilated(
        signal[None],
        kernel[:, None, :],
        (1,),
        "VALID",
        dimension_numbers=("NWC", "WIO", "NWC"),
        feature_group_count=channels,
        preferred_element_type=jnp.float32,
    )
    return result[0]


def select_slot(stacked, slot, live):
    picked = lax.dynamic_index_in_dim(stacked, slot, 0, keepdims=False)
    return jnp.where(live, picked, jnp.zeros_like(picked))


def ring_order(count):
    return list(range(0, count, 2)) + list(range(1, count, 2))[::-1]


def on_device(projected, short_filter, long_filter, skip_gain, out_weight, out_grad, left_source):
    rows_here = projected.shape[1]
    channels = projected.shape[2]
    filt_len = long_filter.shape[0]
    taps = short_filter.shape[1]
    width = out_weight.shape[1]
    ctx_count = lax.axis_size("ctx")
    tp_count = lax.axis_size("tp")
    my_index = lax.axis_index("ctx")
    my_tp = lax.axis_index("tp")
    positions = jnp.arange(ctx_count, dtype=jnp.int32)
    source_raw = left_source[my_index]
    has_left = source_raw >= 0
    source = jnp.maximum(source_raw, 0)
    is_reader = left_source == my_index
    has_right = jnp.any(is_reader)
    reader = jnp.sum(jnp.where(is_reader, positions, 0))
    grad_scale = 1.0 / math.sqrt(rows_here * ctx_count)

    order = ring_order(ctx_count)
    order_table = jnp.array(order, jnp.int32)
    place_table = jnp.array([order.index(i) for i in range(ctx_count)], jnp.int32)
    place = place_table[my_index]
    ahead = [(order[i], order[(i + 1) % ctx_count]) for i in range(ctx_count)]
    behind = [(b, a) for a, b in ahead]
    half_ring = ctx_count // 2
    part = channels // chunk_count

    def owner_of(offset):
        return order_table[lax.rem(place + offset + ctx_count, ctx_count)]

    tail_rows = filt_len + edge_depth
    tail_act = short_forward(projected[:, rows_here - tail_rows :], short_filter, filt_len)
    mixin_tail = (tail_act[1] * tail_act[2]).astype(jnp.bfloat16)
    raw_tail = projected[:, rows_here - edge_depth :].reshape(3 * edge_depth, channels)
    got_tail = lax.all_gather(jnp.concatenate([mixin_tail, raw_tail], 0), "ctx", axis=0)
    left_tail = select_slot(got_tail, source, has_left)
    left_mixin = left_tail[:filt_len]
    left_raw = left_tail[filt_len:].reshape(3, edge_depth, channels)

    arrived = []
    for k in range(chunk_count):
        own = out_weight[k * part : (k + 1) * part]
        up, down = own, own
        if k >= 2:
            up, _ = lax.optimization_barrier((own, arrived[k - 2][-2][2]))
            down, _ = lax.optimization_barrier((own, arrived[k - 2][-1][2]))
        blocks = [(0, 0, own)]
        for step in range(1, half_ring):
            up = lax.ppermute(up, "ctx", ahead)
            down = lax.ppermute(down, "ctx", behind)
            blocks += [(-step, 0, up), (step, 0, down)]
        up = lax.ppermute(up[:, : width // 2], "ctx", ahead)
        down = lax.ppermute(down[:, width // 2 :], "ctx", behind)
        blocks += [(-half_ring, 0, up), (-half_ring, width // 2, down)]
        arrived.append(blocks)

    grad_pieces = [
        lax.dynamic_slice_in_dim(out_grad, owner_of(offset) * width + first, block.shape[1], 1)
        for offset, first, block in arrived[0]
    ]
    mixed_sums = [None] * len(grad_pieces)
    grad_streams_parts, long_parts, short_parts = [], [], []
    for k in range(chunk_count):
        cut = slice(k * part, (k + 1) * part)
        raw = projected[:, :, cut]
        short_taps = short_filter[:, :, cut]
        filt = long_filter[:, cut]
        flipped_taps = jnp.flip(filt, 0)
        skip_row = skip_gain[None, cut]
        act_rest = short_forward(raw, short_taps, rows_here - edge_depth)
        mixin_rest = (act_rest[1] * act_rest[2]).astype(jnp.bfloat16)
        head_rows = filt_len + head_pad
        conv_rest = depthwise(mixin_rest[head_pad + 1 - edge_depth :], flipped_taps)
        streams_ext = jnp.concatenate([left_raw[:, :, cut], raw], 1)
        act_head = short_forward(streams_ext[:, : 2 * edge_depth], short_taps, edge_depth)
        act = jnp.concatenate([act_head, act_rest], 1)
        mixin_head = (act_head[1] * act_head[2]).astype(jnp.bfloat16)
        mixin_ext = jnp.concatenate([left_mixin[:, cut], mixin_head, mixin_rest], 0)
        mixin = mixin_ext[filt_len:]
        conv_head = depthwise(mixin_ext[1 : filt_len + head_rows], flipped_taps)
        conv = jnp.concatenate([conv_head, conv_rest], 0)
        conv = conv + skip_row * mixin.astype(jnp.float32)
        gated = (act[0] * conv).astype(jnp.bfloat16)

        back_grad = None
        for j, (offset, first, block) in enumerate(arrived[k]):
            term = lax.dot_general(
                grad_pieces[j], block, (((1,), (1,)), ((), ())), preferred_element_type=jnp.float32
            )
            back_grad = term if back_grad is None else back_grad + term
            out_term = jnp.dot(gated, block, preferred_element_type=jnp.float32)
            mixed_sums[j] = out_term if k == 0 else mixed_sums[j] + out_term

        grad_conv = (back_grad * act[0]).astype(jnp.bfloat16)
        grad_gate = back_grad * conv
        got_head = lax.all_gather(grad_conv[:filt_len], "ctx", axis=0)
        right_head = select_slot(got_head, reader, has_right)
        mid_rows = rows_here - filt_len
        gm_rest = depthwise(grad_conv[: rows_here - 1], filt)
        gm_tail = depthwise(
            jnp.concatenate([grad_conv[mid_rows:], right_head], 0)[: 2 * filt_len - 1], filt
        )
        grad_mixin = jnp.concatenate([gm_rest, gm_tail], 0)
        grad_mixin = grad_mixin + skip_row * grad_conv.astype(jnp.float32)
        grad_act = jnp.stack([grad_gate, grad_mixin * act[2], grad_mixin * act[1]])
        got_rows = lax.all_gather(
            grad_act[:, :edge_depth].astype(jnp.bfloat16).reshape(3 * edge_depth, part), "ctx", axis=0
        )
        right_rows = select_slot(got_rows, reader, has_right).reshape(3, edge_depth, part)
        grad_act_ext = jnp.concatenate([grad_act, right_rows.astype(jnp.float32)], 1)
        grad_streams = jnp.zeros(grad_act.shape, jnp.float32)
        for shift in range(taps):
            grad_streams = (
                grad_streams
                + short_taps[:, shift][:, None, :] * grad_act_ext[:, shift : shift + rows_here]
            )
        grad_streams_parts.append(grad_streams.astype(jnp.bfloat16))
        short_terms = jnp.stack(
            [
                jnp.sum(
                    grad_act
                    * streams_ext[:, edge_depth - shift : edge_depth - shift + rows_here].astype(
                        jnp.float32
                    ),
                    axis=1,
                )
                for shift in range(taps)
            ],
            axis=1,
        )
        long_terms = depthwise(mixin_ext[1:], grad_conv)
        both = jnp.concatenate(
            [long_terms.astype(jnp.bfloat16), short_terms.reshape(3 * taps, part).astype(jnp.bfloat16)], 0
        )
        total = lax.psum(both, "ctx").astype(jnp.float32) * grad_scale
        long_parts.append(jnp.flip(total[:filt_len], 0))
        short_parts.append(total[filt_len:].reshape(3, taps, part))

    share = rows_here // tp_count
    mixed = jnp.zeros((share, width * ctx_count), jnp.bfloat16)
    for j, (offset, first, block) in enumerate(arrived[0]):
        piece = mixed_sums[j].astype(jnp.bfloat16).reshape(tp_count, share, block.shape[1])
        bit = 1
        while bit < tp_count:
            pairs = piece.reshape(piece.shape[0] // 2, 2, share, block.shape[1])
            mine = lax.rem(my_tp // bit, 2)
            kept = lax.dynamic_index_in_dim(pairs, mine, 1, keepdims=False)
            sent = lax.dynamic_index_in_dim(pairs, 1 - mine, 1, keepdims=False)
            got = lax.ppermute(sent, "tp", [(i, i ^ bit) for i in range(tp_count)])
            piece = (kept.astype(jnp.float32) + got.astype(jnp.float32)).astype(jnp.bfloat16)
            bit *= 2
        mixed = lax.dynamic_update_slice_in_dim(
            mixed, piece[0], owner_of(offset) * width + first, 1
        )
    return (
        mixed,
        jnp.concatenate(grad_streams_parts, 2),
        jnp.concatenate(long_parts, 1),
        jnp.concatenate(short_parts, 2),
    )


def solution(mesh):
    placed = (
        P(None, "ctx", "tp"),
        P(None, None, "tp"),
        P(None, "tp"),
        P("tp"),
        P("tp", "ctx"),
        P("ctx", None),
        P(),
    )
    return jax.shard_map(
        on_device,
        mesh=mesh,
        in_specs=placed,
        out_specs=(
            P(("ctx", "tp"), None),
            P(None, "ctx", "tp"),
            P(None, "tp"),
            P(None, None, "tp"),
        ),
        check_vma=False,
    )
```

```python
import math

import jax
import jax.numpy as jnp
from jax import lax
from jax.sharding import PartitionSpec as P

edge_depth = 8
chunk_count = 4
head_pad = 16


def short_forward(extended, tap_weights, out_rows):
    summed = jnp.zeros((extended.shape[0], out_rows, extended.shape[2]), jnp.float32)
    for shift in range(tap_weights.shape[1]):
        piece = extended[:, edge_depth - shift : edge_depth - shift + out_rows].astype(jnp.float32)
        summed = summed + tap_weights[:, shift][:, None, :] * piece
    return summed


def depthwise(signal, kernel):
    channels = signal.shape[1]
    result = lax.conv_general_dilated(
        signal[None],
        kernel[:, None, :],
        (1,),
        "VALID",
        dimension_numbers=("NWC", "WIO", "NWC"),
        feature_group_count=channels,
        preferred_element_type=jnp.float32,
    )
    return result[0]


def select_slot(stacked, slot, live):
    picked = lax.dynamic_index_in_dim(stacked, slot, 0, keepdims=False)
    return jnp.where(live, picked, jnp.zeros_like(picked))


def ring_order(count):
    return list(range(0, count, 2)) + list(range(1, count, 2))[::-1]


def on_device(projected, short_filter, long_filter, skip_gain, out_weight, out_grad, left_source):
    rows_here = projected.shape[1]
    channels = projected.shape[2]
    filt_len = long_filter.shape[0]
    taps = short_filter.shape[1]
    width = out_weight.shape[1]
    ctx_count = lax.axis_size("ctx")
    tp_count = lax.axis_size("tp")
    my_index = lax.axis_index("ctx")
    my_tp = lax.axis_index("tp")
    positions = jnp.arange(ctx_count, dtype=jnp.int32)
    source_raw = left_source[my_index]
    has_left = source_raw >= 0
    source = jnp.maximum(source_raw, 0)
    is_reader = left_source == my_index
    has_right = jnp.any(is_reader)
    reader = jnp.sum(jnp.where(is_reader, positions, 0))
    grad_scale = 1.0 / math.sqrt(rows_here * ctx_count)

    order = ring_order(ctx_count)
    order_table = jnp.array(order, jnp.int32)
    place_table = jnp.array([order.index(i) for i in range(ctx_count)], jnp.int32)
    place = place_table[my_index]
    ahead = [(order[i], order[(i + 1) % ctx_count]) for i in range(ctx_count)]
    behind = [(b, a) for a, b in ahead]
    half_ring = ctx_count // 2
    part = channels // chunk_count

    def owner_of(offset):
        return order_table[lax.rem(place + offset + ctx_count, ctx_count)]

    tail_rows = filt_len + edge_depth
    tail_act = short_forward(projected[:, rows_here - tail_rows :], short_filter, filt_len)
    mixin_tail = (tail_act[1] * tail_act[2]).astype(jnp.bfloat16)
    raw_tail = projected[:, rows_here - edge_depth :].reshape(3 * edge_depth, channels)
    got_tail = lax.all_gather(jnp.concatenate([mixin_tail, raw_tail], 0), "ctx", axis=0)
    left_tail = select_slot(got_tail, source, has_left)
    left_mixin = left_tail[:filt_len]
    left_raw = left_tail[filt_len:].reshape(3, edge_depth, channels)

    arrived, rest_convs, lag_terms = [], [], []

    def gather_chunk(k):
        own = out_weight[k * part : (k + 1) * part]
        up, down = own, own
        if k >= 2:
            up, _ = lax.optimization_barrier((own, arrived[k - 2][-2][2]))
            down, _ = lax.optimization_barrier((own, arrived[k - 2][-1][2]))
        blocks = [(0, 0, own)]
        for step in range(1, half_ring):
            if k >= 2 and step == 2:
                up, rest_convs[k - 2] = lax.optimization_barrier((up, rest_convs[k - 2]))
            if k >= 2 and step == half_ring - 1:
                down, lag_terms[k - 2] = lax.optimization_barrier((down, lag_terms[k - 2]))
            up = lax.ppermute(up, "ctx", ahead)
            down = lax.ppermute(down, "ctx", behind)
            blocks += [(-step, 0, up), (step, 0, down)]
        up = lax.ppermute(up[:, : width // 2], "ctx", ahead)
        down = lax.ppermute(down[:, width // 2 :], "ctx", behind)
        blocks += [(-half_ring, 0, up), (-half_ring, width // 2, down)]
        arrived.append(blocks)

    gather_chunk(0)
    grad_pieces = [
        lax.dynamic_slice_in_dim(out_grad, owner_of(offset) * width + first, block.shape[1], 1)
        for offset, first, block in arrived[0]
    ]
    mixed_sums = [None] * len(grad_pieces)
    grad_streams_parts, long_parts, short_parts = [], [], []
    kept_values = []
    for k in range(chunk_count):
        if k + 1 < chunk_count:
            gather_chunk(k + 1)
        cut = slice(k * part, (k + 1) * part)
        raw = projected[:, :, cut]
        short_taps = short_filter[:, :, cut]
        filt = long_filter[:, cut]
        flipped_taps = jnp.flip(filt, 0)
        skip_row = skip_gain[None, cut]
        act_rest = short_forward(raw, short_taps, rows_here - edge_depth)
        mixin_rest = (act_rest[1] * act_rest[2]).astype(jnp.bfloat16)
        head_rows = filt_len + head_pad
        conv_rest = depthwise(mixin_rest[head_pad + 1 - edge_depth :], flipped_taps)
        streams_ext = jnp.concatenate([left_raw[:, :, cut], raw], 1)
        act_head = short_forward(streams_ext[:, : 2 * edge_depth], short_taps, edge_depth)
        act = jnp.concatenate([act_head, act_rest], 1)
        mixin_head = (act_head[1] * act_head[2]).astype(jnp.bfloat16)
        mixin_ext = jnp.concatenate([left_mixin[:, cut], mixin_head, mixin_rest], 0)
        mixin = mixin_ext[filt_len:]
        conv_head = depthwise(mixin_ext[1 : filt_len + head_rows], flipped_taps)
        conv = jnp.concatenate([conv_head, conv_rest], 0)
        conv = conv + skip_row * mixin.astype(jnp.float32)
        gated = (act[0] * conv).astype(jnp.bfloat16)

        back_grad = None
        for j, (offset, first, block) in enumerate(arrived[k]):
            term = lax.dot_general(
                grad_pieces[j], block, (((1,), (1,)), ((), ())), preferred_element_type=jnp.float32
            )
            back_grad = term if back_grad is None else back_grad + term
            out_term = jnp.dot(gated, block, preferred_element_type=jnp.float32)
            mixed_sums[j] = out_term if k == 0 else mixed_sums[j] + out_term

        grad_conv = (back_grad * act[0]).astype(jnp.bfloat16)
        grad_gate = back_grad * conv
        rest_convs.append(depthwise(grad_conv[: rows_here - 1], filt))
        lag_terms.append(depthwise(mixin_ext[1:], grad_conv))
        kept_values.append((act, grad_conv, grad_gate, streams_ext))

    heads = jnp.concatenate([values[1][:filt_len] for values in kept_values], 1)
    right_heads = select_slot(lax.all_gather(heads, "ctx", axis=0), reader, has_right)
    mid_rows = rows_here - filt_len
    grad_acts = []
    for k in range(chunk_count):
        cut = slice(k * part, (k + 1) * part)
        act, grad_conv, grad_gate, streams_ext = kept_values[k]
        filt = long_filter[:, cut]
        skip_row = skip_gain[None, cut]
        gm_rest, right_head = rest_convs[k], right_heads[:, cut]
        gm_tail = depthwise(
            jnp.concatenate([grad_conv[mid_rows:], right_head], 0)[: 2 * filt_len - 1], filt
        )
        grad_mixin = jnp.concatenate([gm_rest, gm_tail], 0)
        grad_mixin = grad_mixin + skip_row * grad_conv.astype(jnp.float32)
        grad_act = jnp.stack([grad_gate, grad_mixin * act[2], grad_mixin * act[1]])
        grad_acts.append(grad_act)

    share = rows_here // tp_count
    mixed = jnp.zeros((share, width * ctx_count), jnp.bfloat16)
    for j, (offset, first, block) in enumerate(arrived[0]):
        piece = mixed_sums[j].astype(jnp.bfloat16).reshape(tp_count, share, block.shape[1])
        bit = 1
        while bit < tp_count:
            pairs = piece.reshape(piece.shape[0] // 2, 2, share, block.shape[1])
            mine = lax.rem(my_tp // bit, 2)
            kept = lax.dynamic_index_in_dim(pairs, mine, 1, keepdims=False)
            sent = lax.dynamic_index_in_dim(pairs, 1 - mine, 1, keepdims=False)
            got = lax.ppermute(sent, "tp", [(i, i ^ bit) for i in range(tp_count)])
            piece = (kept.astype(jnp.float32) + got.astype(jnp.float32)).astype(jnp.bfloat16)
            bit *= 2
        mixed = lax.dynamic_update_slice_in_dim(
            mixed, piece[0], owner_of(offset) * width + first, 1
        )
    edge_grads = jnp.concatenate(
        [g[:, :edge_depth].astype(jnp.bfloat16).reshape(3 * edge_depth, part) for g in grad_acts], 1
    )
    edge_grads, mixed = lax.optimization_barrier((edge_grads, mixed))
    right_edges = select_slot(lax.all_gather(edge_grads, "ctx", axis=0), reader, has_right)
    right_edges = right_edges.reshape(3, edge_depth, channels)
    for k in range(chunk_count):
        cut = slice(k * part, (k + 1) * part)
        short_taps = short_filter[:, :, cut]
        grad_act, streams_ext, right_rows = grad_acts[k], kept_values[k][3], right_edges[:, :, cut]
        grad_act_ext = jnp.concatenate([grad_act, right_rows.astype(jnp.float32)], 1)
        grad_streams = jnp.zeros(grad_act.shape, jnp.float32)
        for shift in range(taps):
            grad_streams = (
                grad_streams
                + short_taps[:, shift][:, None, :] * grad_act_ext[:, shift : shift + rows_here]
            )
        grad_streams_parts.append(grad_streams.astype(jnp.bfloat16))
        short_terms = jnp.stack(
            [
                jnp.sum(
                    grad_act
                    * streams_ext[:, edge_depth - shift : edge_depth - shift + rows_here].astype(
                        jnp.float32
                    ),
                    axis=1,
                )
                for shift in range(taps)
            ],
            axis=1,
        )
        long_terms = lag_terms[k]
        both = jnp.concatenate(
            [long_terms.astype(jnp.bfloat16), short_terms.reshape(3 * taps, part).astype(jnp.bfloat16)], 0
        )
        total = lax.psum(both, "ctx").astype(jnp.float32) * grad_scale
        long_parts.append(jnp.flip(total[:filt_len], 0))
        short_parts.append(total[filt_len:].reshape(3, taps, part))

    return (
        mixed,
        jnp.concatenate(grad_streams_parts, 2),
        jnp.concatenate(long_parts, 1),
        jnp.concatenate(short_parts, 2),
    )


def solution(mesh):
    placed = (
        P(None, "ctx", "tp"),
        P(None, None, "tp"),
        P(None, "tp"),
        P("tp"),
        P("tp", "ctx"),
        P("ctx", None),
        P(),
    )
    return jax.shard_map(
        on_device,
        mesh=mesh,
        in_specs=placed,
        out_specs=(
            P(("ctx", "tp"), None),
            P(None, "ctx", "tp"),
            P(None, "tp"),
            P(None, None, "tp"),
        ),
        check_vma=False,
    )
```
